32 devices in a mesh: groups: 2 (over y), row: 4 (over z), col: 2 (over x), rep: 2 (over core).
Axes of the slice: x: 2, y: 2, z: 4, core: 2. Of those that a mesh axis runs over, the one named last changes fastest.
Arguments:
- density: float32 [256, 64, 64], P(('groups', 'row', 'col', 'rep')), parts along dimension 0, may hold values from -0.09 to 0.09
- left_index: int32 [2, 2, 256, 32], P(None, None, ('groups', 'row', 'col', 'rep')), parts along dimension 2, may hold values from 0 to 31
- right_index: int32 [2, 2, 256, 32], P(None, None, ('groups', 'row', 'col', 'rep')), parts along dimension 2, may hold values from 0 to 63
- pair_count: int32 [2, 2, 256], P(None, None, ('groups', 'row', 'col', 'rep')), parts along dimension 2, may hold values from 8 to 32, as said below
Outputs:
- purified: float32 [256, 64, 64], P(('groups', 'row', 'col', 'rep')), parts along dimension 0
The draws below stay inside these ranges and needn't reach their ends.
There are 2 independent parts, one for each index of `groups`. The reference program is written for one: setup_inputs(seed, part) draws one part's arguments, and reference() takes and returns one part's arrays. A program takes and returns all parts, laid end to end along the dimension named above; each array names one. Nothing has to cross between parts.
Inputs may be any that keep to these rules, and one draw needn't show every extreme that they name: `pair_count`: each aligned group of 8 stored blocks has, for every step and product, one block with all 32 pairs live.
All inputs are finite; a program needn't handle non-finite values.
Results may differ from the reference program's by a relative error of at most 0.0003.
Values sent between devices are 32-bit elements; how exact they have to be, the bound alone decides.
No kernel may reach another device: no remote copies, remote signals or barrier semaphores. Data moves between devices by JAX's collectives and lax.ppermute only.
A program may use at most 128 MiB of HBM per device.

```python
import jax
import jax.numpy as jnp
from jax import lax

BLK = 64
SLOT_DEV = 8
PAIRS = 32
STEPS = 2
SLOTS = 128
ROW_PANEL = 32
COL_PANEL = 64
N_ROW = 4
N_COL = 2
N_REP = 2


def draw_pair_count(key, part):
    key = jax.random.fold_in(key, 7)
    first, second = jax.random.split(key)
    counts = jax.random.randint(first, (STEPS, 2, SLOTS), PAIRS // 4, PAIRS + 1, dtype=jnp.int32)
    full_at = jax.random.randint(second, (STEPS, 2, SLOTS // SLOT_DEV, 1), 0, SLOT_DEV, dtype=jnp.int32)
    position = jnp.arange(SLOTS, dtype=jnp.int32).reshape(SLOTS // SLOT_DEV, SLOT_DEV) % SLOT_DEV
    filled = jnp.where(position[None, None] == full_at, PAIRS, counts.reshape(STEPS, 2, SLOTS // SLOT_DEV, SLOT_DEV))
    return filled.reshape(STEPS, 2, SLOTS).astype(jnp.int32)


def set_ends(values, rng, low, largest):
    shape = values.shape
    spot = [jax.random.randint(jax.random.fold_in(rng, axis), (), 0, shape[axis]) for axis in range(len(shape))]
    values = values.at[tuple(spot)].set(low)
    longest = shape.index(max(shape))
    spot[longest] = (spot[longest] + 1) % shape[longest]
    return values.at[tuple(spot)].set(largest)


def steps_of(stream_key, extent, cuts, smallest, high):
    loudness = 1.0
    for axis_at, parts in cuts:
        steps = jax.random.uniform(jax.random.fold_in(jax.random.fold_in(stream_key, 6), axis_at), (parts,), jnp.float32, smallest / len(cuts), high / len(cuts))
        loudness = loudness * jnp.repeat(jnp.exp(steps), extent[axis_at] // parts).reshape((-1,) + (1,) * (len(extent) - 1 - axis_at))
    return loudness


def gaussian(own_key, extent, spread, limit, cuts=(), held_as=jnp.bfloat16):
    array = jax.random.normal(own_key, extent, jnp.float32) * spread
    if len(cuts) > 0:
        array = steps_of(own_key, extent, cuts, -0.22, 0.18) * array
    return jnp.clip(array, min=-limit, max=limit).astype(held_as)


def setup_inputs(seed: int = 0, part: int = 0) -> dict:
    key_list = jax.random.split(jax.random.key(seed), 5)
    part_keys = jax.random.split(jax.random.fold_in(key_list[4], part), 5)
    density = gaussian(part_keys[0], (SLOTS, BLK, BLK), 0.015625, 0.09, ((0, 16),), jnp.float32)
    left_index = set_ends(jax.random.randint(part_keys[1], (STEPS, 2, SLOTS, PAIRS), 0, ROW_PANEL), jax.random.fold_in(part_keys[1], 1), 0, ROW_PANEL - 1).astype(jnp.int32)
    right_index = set_ends(jax.random.randint(part_keys[2], (STEPS, 2, SLOTS, PAIRS), 0, COL_PANEL), jax.random.fold_in(part_keys[2], 1), 0, COL_PANEL - 1).astype(jnp.int32)
    pair_count = draw_pair_count(jax.random.fold_in(jax.random.fold_in(key_list[4], part), 71), part)
    return dict(density=density, left_index=left_index, right_index=right_index, pair_count=pair_count)


def multiply(left, right, left_rows, right_rows, live_counts):
    left_panels = left.reshape(N_ROW, N_COL * N_REP * SLOT_DEV, BLK, BLK)
    right_grid = right.reshape(N_ROW, N_COL, N_REP, SLOT_DEV, BLK, BLK)
    right_panels = jnp.transpose(right_grid, (1, 0, 2, 3, 4, 5)).reshape(N_COL, N_ROW * N_REP * SLOT_DEV, BLK, BLK)
    left_tiles = left_rows.reshape(N_ROW, N_COL, N_REP * SLOT_DEV, PAIRS)
    right_tiles = right_rows.reshape(N_ROW, N_COL, N_REP * SLOT_DEV, PAIRS)
    count_tiles = live_counts.reshape(N_ROW, N_COL, N_REP * SLOT_DEV)

    def one_tile(flat):
        row_at = flat // N_COL
        col_at = flat % N_COL
        left_blocks = jnp.take(left_panels[row_at], left_tiles[row_at, col_at], axis=0)
        right_blocks = jnp.take(right_panels[col_at], right_tiles[row_at, col_at], axis=0)
        positions = jnp.arange(PAIRS, dtype=jnp.int32)
        live = positions[None, :] < count_tiles[row_at, col_at][:, None]
        left_blocks = jnp.where(live[:, :, None, None], left_blocks, jnp.zeros_like(left_blocks))
        return jnp.einsum('tkij,tkjl->til', left_blocks, right_blocks, precision=lax.Precision.HIGHEST)

    result = lax.map(one_tile, jnp.arange(N_ROW * N_COL, dtype=jnp.int32))
    return result.reshape(SLOTS, BLK, BLK)


def reference(density, left_index, right_index, pair_count):
    current = density
    for step in range(STEPS):
        square = multiply(current, current, left_index[step, 0], right_index[step, 0], pair_count[step, 0])
        cube = multiply(square, current, left_index[step, 1], right_index[step, 1], pair_count[step, 1])
        current = 3.0 * square - 2.0 * cube
    return current
```

```python
import functools

import jax
import jax.numpy as jnp
from jax import lax
from jax.experimental import pallas as pl
from jax.experimental.pallas import tpu as pltpu
from jax.sharding import PartitionSpec as P

STEPS = 2
CODE = 256
CHUNK = 4
VMEM = pl.BlockSpec(memory_space=pltpu.VMEM)
ANY = pl.BlockSpec(memory_space=pl.ANY)
BF16 = jnp.bfloat16
F32 = jnp.float32


def middle_view(blocks):
    width = blocks.shape[1]
    padded = jnp.concatenate([blocks, jnp.zeros((1, width, width), blocks.dtype)], axis=0)
    return jnp.transpose(padded, (1, 0, 2))


def multiply(left_blocks, right_blocks, left_rows, right_rows, live_counts):
    slot_count, pair_width = left_rows.shape
    width = left_blocks.shape[1]
    left_view = middle_view(left_blocks)
    right_view = middle_view(right_blocks)
    positions = jnp.arange(pair_width, dtype=jnp.int32)
    live = positions[None, :] < live_counts[:, None]
    left_pick = jnp.where(live, left_rows, left_blocks.shape[0]).reshape(slot_count * pair_width)
    right_pick = jnp.where(live, right_rows, right_blocks.shape[0]).reshape(slot_count * pair_width)
    left_taken = jnp.take(left_view, left_pick, axis=1).reshape(
        width, slot_count, pair_width, width
    )
    right_taken = jnp.take(right_view, right_pick, axis=1).reshape(
        width, slot_count, pair_width, width
    )
    return jnp.einsum("iskj,jskl->sil", left_taken, right_taken, precision=lax.Precision.HIGHEST)


def panel_form(density, left_index, right_index, pair_count):
    current = density
    for step in range(STEPS):
        row_blocks = lax.all_gather(current, ("col", "rep"), axis=0, tiled=True)
        column_blocks = lax.all_gather(current, ("row", "rep"), axis=0, tiled=True)
        square = multiply(
            row_blocks,
            column_blocks,
            left_index[step, 0],
            right_index[step, 0],
            pair_count[step, 0],
        )
        square_rows = lax.all_gather(square, ("col", "rep"), axis=0, tiled=True)
        cube = multiply(
            square_rows,
            column_blocks,
            left_index[step, 1],
            right_index[step, 1],
            pair_count[step, 1],
        )
        current = 3.0 * square - 2.0 * cube
    return current


def left_lanes(rows):
    return lax.broadcasted_iota(jnp.int32, (rows, 128), 1) < 64


def spread(packed):
    turned = pltpu.roll(packed, 64, 1)
    left = left_lanes(32)
    return jnp.concatenate([jnp.where(left, packed, turned), jnp.where(left, turned, packed)], axis=0)


def pack(twice):
    return jnp.where(left_lanes(32), twice[:32], twice[32:])


def halves(twice):
    high = twice.astype(BF16)
    return high, twice - high.astype(F32)


def store_left(ref, at, twice):
    high, low = halves(twice)
    ref[at, 0:64] = high
    ref[at, 64:128] = low.astype(BF16)


def store_right(ref, at, twice):
    high, low = halves(twice)
    ref[at] = jnp.where(left_lanes(64), high.astype(F32), low).astype(BF16)


def prepare(source, first, count, base, left_ref, right_ref, unroll=8):
    def body(i, carry):
        twice = spread(source[first + i])
        if left_ref is not None:
            store_left(left_ref, base + i, twice)
        if right_ref is not None:
            store_right(right_ref, base + i, twice)
        return carry

    lax.fori_loop(0, count, body, 0, unroll=unroll)


def zero_block(left_ref, left_at, right_ref, right_at):
    if left_ref is not None:
        left_ref[left_at] = jnp.zeros((128, 128), BF16)
    if right_ref is not None:
        right_ref[right_at] = jnp.zeros((64, 128), BF16)


def filtered(codes, at, lane, pairs, left_ref, right_ref):
    mask = left_lanes(128)
    total = jnp.zeros((128, 128), F32)
    for start in range(0, pairs, CHUNK):
        lefts, rights = [], []
        for p in range(start, start + CHUNK):
            code = codes[at, lane + p]
            lefts.append(left_ref[(code >> 8) & (CODE - 1)])
            rights.append(right_ref[code & (CODE - 1)])
        left = jnp.concatenate(
            [jnp.where(mask, lefts[0], lefts[1]), jnp.where(mask, lefts[2], lefts[3])], axis=1
        )
        right = jnp.concatenate(rights, axis=0)
        total = total + jnp.dot(left, right, preferred_element_type=F32)
    both = total[:64] + total[64:]
    return both + pltpu.roll(both, 64, 1)


class Sizes:
    def __init__(self, mesh_shape, slots, pairs):
        self.rows, self.cols, self.reps = mesh_shape["row"], mesh_shape["col"], mesh_shape["rep"]
        self.slots, self.pairs = slots, pairs
        self.tile = self.reps * slots
        self.panel = self.cols * self.tile
        self.tiles = self.rows * self.cols
        self.blocks = self.tiles * self.tile
        self.half = self.tiles * slots


def pack_kernel(sizes, density, left_index, right_index, pair_count, out, blocks, lefts, rights, counts, sems):
    copies = [
        pltpu.make_async_copy(source, target, sems.at[i])
        for i, (source, target) in enumerate(
            ((density, blocks), (left_index, lefts), (right_index, rights), (pair_count, counts))
        )
    ]
    for copy in copies:
        copy.start()
    row, col = lax.axis_index("row"), lax.axis_index("col")
    for copy in copies[1:]:
        copy.wait()
    position = lax.broadcasted_iota(jnp.int32, (sizes.slots, sizes.pairs), 1)
    slot = lax.broadcasted_iota(jnp.int32, (sizes.slots, sizes.pairs), 0)
    codes = []
    for n in range(STEPS):
        for q in range(2):
            live = jnp.zeros((sizes.slots, sizes.pairs), jnp.int32)
            for s in range(sizes.slots):
                live = jnp.where(slot == s, counts[n, q, s], live)
            right = rights[n, q]
            inside = lax.rem(right, sizes.tile)
            left = lefts[n, q] + (row * sizes.panel if n == 0 else 0)
            right = (right - inside) * sizes.cols + col * sizes.tile + inside
            dead = position >= live
            left = jnp.where(dead, sizes.blocks if n == 0 else sizes.panel, left)
            right = jnp.where(dead, sizes.blocks, right)
            codes.append(((live * CODE + left) * CODE + right).astype(F32))
    out[sizes.slots * 32 : sizes.slots * 33] = jnp.concatenate(codes, axis=1)
    copies[0].wait()
    for s in range(sizes.slots):
        out[s * 32 : s * 32 + 32] = jnp.concatenate([blocks[s, :32], blocks[s, 32:]], axis=1)


def first_square_kernel(sizes, *refs):
    count = sizes.tiles * sizes.reps
    pieces, (out, right_ref, codes_out, left_ref, codes, sem) = refs[:count], refs[count:]
    row, col, rep = lax.axis_index("row"), lax.axis_index("col"), lax.axis_index("rep")
    places = []
    for e in range(sizes.reps):
        for m in range(sizes.rows):
            for n in range(sizes.cols):
                tile = (row ^ m) * sizes.cols + (col ^ n)
                places.append(pl.multiple_of(tile * sizes.tile + (rep ^ e) * sizes.slots, sizes.slots))
    for piece, base in zip(pieces, places):
        codes_out[pl.ds(base, sizes.slots)] = piece[sizes.slots * 32 : sizes.slots * 33].astype(jnp.int32)
    copy = pltpu.make_async_copy(codes_out, codes, sem)
    copy.start()
    zero_block(left_ref, sizes.blocks, right_ref, sizes.blocks)
    for piece, base in zip(pieces, places):
        for s in range(sizes.slots):
            twice = spread(piece[s * 32 : s * 32 + 32])
            store_left(left_ref, base + s, twice)
            store_right(right_ref, base + s, twice)
    copy.wait()

    def body(i, carry):
        base = (i * sizes.reps + rep) * sizes.slots
        for s in range(sizes.slots):
            out[i * sizes.slots + s] = pack(filtered(codes, base + s, 0, sizes.pairs, left_ref, right_ref))
        return carry

    lax.fori_loop(0, sizes.tiles, body, 0)


def first_cube_kernel(sizes, own, other, right_ref, codes_in, out, left_ref, codes, sem):
    copy = pltpu.make_async_copy(codes_in, codes, sem)
    copy.start()
    rep = lax.axis_index("rep")
    zero_block(left_ref, sizes.blocks, None, None)

    def prepare_tile(i, carry):
        for e, source in ((rep, own), (1 - rep, other)):
            for s in range(sizes.slots):
                store_left(
                    left_ref, (i * sizes.reps + e) * sizes.slots + s, spread(source[i * sizes.slots + s])
                )
        return carry

    lax.fori_loop(0, sizes.tiles, prepare_tile, 0)
    copy.wait()

    def body(i, carry):
        base = (i * sizes.reps + rep) * sizes.slots
        for s in range(sizes.slots):
            cube = pack(filtered(codes, base + s, sizes.pairs, sizes.pairs, left_ref, right_ref))
            out[i * sizes.slots + s] = 3.0 * own[i * sizes.slots + s] - 2.0 * cube
        return carry

    lax.fori_loop(0, sizes.tiles, body, 0)


def last_square_kernel(sizes, own, other, codes_in, out, right_ref, left_ref, codes, sem):
    copy = pltpu.make_async_copy(codes_in, codes, sem)
    copy.start()
    row, rep = lax.axis_index("row"), lax.axis_index("rep")
    zero_block(left_ref, sizes.panel, right_ref, sizes.blocks)

    def prepare_tile(i, carry):
        for e, source in ((rep, own), (1 - rep, other)):
            for s in range(sizes.slots):
                store_right(
                    right_ref, (i * sizes.reps + e) * sizes.slots + s, spread(source[i * sizes.slots + s])
                )
        return carry

    lax.fori_loop(0, sizes.tiles, prepare_tile, 0)
    for n in range(sizes.cols):
        for e, source in ((rep, own), (1 - rep, other)):
            for s in range(sizes.slots):
                twice = spread(source[(row * sizes.cols + n) * sizes.slots + s])
                store_left(left_ref, (n * sizes.reps + e) * sizes.slots + s, twice)
    copy.wait()

    def body(n, carry):
        base = row * sizes.panel + (n * sizes.reps + rep) * sizes.slots
        for s in range(sizes.slots):
            out[n * sizes.slots + s] = pack(
                filtered(codes, base + s, 2 * sizes.pairs, sizes.pairs, left_ref, right_ref)
            )
        return carry

    lax.fori_loop(0, sizes.cols, body, 0)


def last_cube_kernel(sizes, own, other, right_ref, codes_in, out, left_ref, codes, sem):
    copy = pltpu.make_async_copy(codes_in, codes, sem)
    copy.start()
    row, col, rep = lax.axis_index("row"), lax.axis_index("col"), lax.axis_index("rep")
    zero_block(left_ref, sizes.panel, None, None)
    for n in range(sizes.cols):
        for e, source in ((rep, own), (1 - rep, other)):
            for s in range(sizes.slots):
                twice = spread(source[n * sizes.slots + s])
                store_left(left_ref, (n * sizes.reps + e) * sizes.slots + s, twice)
    copy.wait()
    base = row * sizes.panel + (col * sizes.reps + rep) * sizes.slots
    for s in range(sizes.slots):
        cube = filtered(codes, base + s, 3 * sizes.pairs, sizes.pairs, left_ref, right_ref)
        square = spread(own[col * sizes.slots + s])
        out[s] = (3.0 * square - 2.0 * cube)[:, :64]


def call(kernel, sizes, outs, in_specs, out_specs, scratch, limit=40):
    return pl.pallas_call(
        functools.partial(kernel, sizes),
        out_shape=outs,
        in_specs=in_specs,
        out_specs=out_specs,
        scratch_shapes=scratch,
        compiler_params=pltpu.CompilerParams(vmem_limit_bytes=limit * 2**20),
    )


def whole_form(sizes, density, left_index, right_index, pair_count):
    width = density.shape[1]
    index_shape = (STEPS, 2, sizes.slots, sizes.pairs)
    code_shape = (sizes.blocks, STEPS * 2 * sizes.pairs)
    packed = lambda count: jax.ShapeDtypeStruct((count, 32, 128), F32)
    rights = jax.ShapeDtypeStruct((sizes.blocks + 1, 64, 128), BF16)
    code_scratch = [pltpu.SMEM(code_shape, jnp.int32), pltpu.SemaphoreType.DMA]

    payload = call(
        pack_kernel,
        sizes,
        jax.ShapeDtypeStruct((sizes.slots * 33, 128), F32),
        [ANY] * 4,
        VMEM,
        [
            pltpu.VMEM((sizes.slots, width, width), F32),
            pltpu.VMEM(index_shape, jnp.int32),
            pltpu.VMEM(index_shape, jnp.int32),
            pltpu.SMEM((STEPS, 2, sizes.slots), jnp.int32),
            pltpu.SemaphoreType.DMA((4,)),
        ],
    )(density, left_index, right_index, pair_count)

    def row_swap(value, m):
        return lax.ppermute(value, "row", [(i, i ^ m) for i in range(sizes.rows)])

    def both_swap(value, m):
        axes = ("row", "col")
        return lax.ppermute(value, axes, [(i, i ^ (2 * m + 1)) for i in range(2 * sizes.rows)])

    def col_swap(value):
        return lax.ppermute(value, "col", [(0, 1), (1, 0)])

    def rep_swap(value):
        return lax.ppermute(value, "rep", [(0, 1), (1, 0)])

    pieces = [payload, col_swap(payload)]
    for m in range(1, sizes.rows):
        arrived = row_swap(payload, m)
        pieces += [arrived, both_swap(payload, m) if m == 1 else col_swap(arrived)]
    pieces += [rep_swap(piece) for piece in pieces]

    square, right, codes = call(
        first_square_kernel,
        sizes,
        [packed(sizes.half), rights, jax.ShapeDtypeStruct(code_shape, jnp.int32)],
        [VMEM] * len(pieces),
        [VMEM] * 3,
        [pltpu.VMEM((sizes.blocks + 1, 128, 128), BF16)] + code_scratch,
    )(*pieces)
    current = call(
        first_cube_kernel,
        sizes,
        packed(sizes.half),
        [VMEM] * 3 + [ANY],
        VMEM,
        [pltpu.VMEM((sizes.blocks + 1, 128, 128), BF16)] + code_scratch,
    )(square, rep_swap(square), right, codes)
    square, right = call(
        last_square_kernel,
        sizes,
        [packed(sizes.cols * sizes.slots), rights],
        [VMEM] * 2 + [ANY],
        [VMEM] * 2,
        [pltpu.VMEM((sizes.panel + 1, 128, 128), BF16)] + code_scratch,
    )(current, rep_swap(current), codes)
    return call(
        last_cube_kernel,
        sizes,
        jax.ShapeDtypeStruct(density.shape, F32),
        [VMEM] * 3 + [ANY],
        VMEM,
        [pltpu.VMEM((sizes.panel + 1, 128, 128), BF16)] + code_scratch,
    )(square, rep_swap(square), right, codes)


def solution(mesh):
    def local(density, left_index, right_index, pair_count):
        sizes = Sizes(mesh.shape, density.shape[0], left_index.shape[3])
        fits = (
            sizes.blocks + 1 <= CODE
            and sizes.rows & (sizes.rows - 1) == 0
            and (sizes.cols, sizes.reps, sizes.slots, sizes.pairs) == (2, 2, 8, 32)
            and density.shape[1:] == (64, 64)
        )
        if fits:
            return whole_form(sizes, density, left_index, right_index, pair_count)
        return panel_form(density, left_index, right_index, pair_count)

    in_specs = (
        P(("groups", "row", "col", "rep"), None, None),
        P(None, None, ("groups", "row", "col", "rep"), None),
        P(None, None, ("groups", "row", "col", "rep"), None),
        P(None, None, ("groups", "row", "col", "rep")),
    )
    out_specs = P(("groups", "row", "col", "rep"), None, None)
    return jax.shard_map(local, mesh=mesh, in_specs=in_specs, out_specs=out_specs, check_vma=False)
```

```python
import functools

import jax
import jax.numpy as jnp
from jax import lax
from jax.experimental import pallas as pl
from jax.experimental.pallas import tpu as pltpu
from jax.sharding import PartitionSpec as P

STEPS = 2
CODE = 256
CHUNK = 4
VMEM = pl.BlockSpec(memory_space=pltpu.VMEM)
ANY = pl.BlockSpec(memory_space=pl.ANY)
BF16 = jnp.bfloat16
F32 = jnp.float32


def middle_view(blocks):
    width = blocks.shape[1]
    padded = jnp.concatenate([blocks, jnp.zeros((1, width, width), blocks.dtype)], axis=0)
    return jnp.transpose(padded, (1, 0, 2))


def multiply(left_blocks, right_blocks, left_rows, right_rows, live_counts):
    slot_count, pair_width = left_rows.shape
    width = left_blocks.shape[1]
    left_view = middle_view(left_blocks)
    right_view = middle_view(right_blocks)
    positions = jnp.arange(pair_width, dtype=jnp.int32)
    live = positions[None, :] < live_counts[:, None]
    left_pick = jnp.where(live, left_rows, left_blocks.shape[0]).reshape(slot_count * pair_width)
    right_pick = jnp.where(live, right_rows, right_blocks.shape[0]).reshape(slot_count * pair_width)
    left_taken = jnp.take(left_view, left_pick, axis=1).reshape(
        width, slot_count, pair_width, width
    )
    right_taken = jnp.take(right_view, right_pick, axis=1).reshape(
        width, slot_count, pair_width, width
    )
    return jnp.einsum("iskj,jskl->sil", left_taken, right_taken, precision=lax.Precision.HIGHEST)


def panel_form(density, left_index, right_index, pair_count):
    current = density
    for step in range(STEPS):
        row_blocks = lax.all_gather(current, ("col", "rep"), axis=0, tiled=True)
        column_blocks = lax.all_gather(current, ("row", "rep"), axis=0, tiled=True)
        square = multiply(
            row_blocks,
            column_blocks,
            left_index[step, 0],
            right_index[step, 0],
            pair_count[step, 0],
        )
        square_rows = lax.all_gather(square, ("col", "rep"), axis=0, tiled=True)
        cube = multiply(
            square_rows,
            column_blocks,
            left_index[step, 1],
            right_index[step, 1],
            pair_count[step, 1],
        )
        current = 3.0 * square - 2.0 * cube
    return current


def left_lanes(rows):
    return lax.broadcasted_iota(jnp.int32, (rows, 128), 1) < 64


def spread(packed):
    turned = pltpu.roll(packed, 64, 1)
    left = left_lanes(32)
    return jnp.concatenate([jnp.where(left, packed, turned), jnp.where(left, turned, packed)], axis=0)


def pack(twice):
    return jnp.where(left_lanes(32), twice[:32], twice[32:])


def halves(twice):
    high = twice.astype(BF16)
    return high, twice - high.astype(F32)


def store_left(ref, at, twice):
    high, low = halves(twice)
    ref[at, 0:64] = high
    ref[at, 64:128] = low.astype(BF16)


def store_right(ref, at, twice):
    high, low = halves(twice)
    ref[at] = jnp.where(left_lanes(64), high.astype(F32), low).astype(BF16)


def prepare(source, first, count, base, left_ref, right_ref, unroll=8):
    def body(i, carry):
        twice = spread(source[first + i])
        if left_ref is not None:
            store_left(left_ref, base + i, twice)
        if right_ref is not None:
            store_right(right_ref, base + i, twice)
        return carry

    lax.fori_loop(0, count, body, 0, unroll=unroll)


def zero_block(left_ref, left_at, right_ref, right_at):
    if left_ref is not None:
        left_ref[left_at] = jnp.zeros((128, 128), BF16)
    if right_ref is not None:
        right_ref[right_at] = jnp.zeros((64, 128), BF16)


def block_products(codes, at, lane, pairs, left_ref, right_ref):
    mask = left_lanes(128)
    total = jnp.zeros((128, 128), F32)
    for start in range(0, pairs, CHUNK):
        lefts, rights = [], []
        for p in range(start, start + CHUNK):
            code = codes[at, lane + p]
            lefts.append(left_ref[(code >> 8) & (CODE - 1)])
            rights.append(right_ref[code & (CODE - 1)])
        left = jnp.concatenate(
            [jnp.where(mask, lefts[0], lefts[1]), jnp.where(mask, lefts[2], lefts[3])], axis=1
        )
        right = jnp.concatenate(rights, axis=0)
        total = total + jnp.dot(left, right, preferred_element_type=F32)
    return total


def fold(total):
    both = total[:64] + total[64:]
    return both + pltpu.roll(both, 64, 1)


def ordered_products(sizes, codes, line, first, product, blocks, group, left_ref, right_ref, finish):
    lane = product * sizes.pairs
    limits = (0, sizes.pairs // 2, 3 * sizes.pairs // 4, sizes.pairs)

    def body(g, carry):
        most = codes[line + product, g * group] >> 8
        for low, high in zip(limits[:-1], limits[1:]):

            @pl.when((most > low) & (most <= high))
            def _():
                for s in range(group):
                    place = (codes[line + product, g * group + s] & (CODE - 1)) - first
                    finish(place, fold(block_products(codes, place, lane, high, left_ref, right_ref)))

        return carry

    lax.fori_loop(0, blocks // group, body, 0)


def order_by_count(codes, lane, wanted, blocks):
    block = lax.broadcasted_iota(jnp.int32, (blocks, 128), 0)
    count = jnp.broadcast_to(codes[:, lane : lane + 1] >> 16, (blocks, 128))
    key = jnp.where(wanted(block), count * CODE + block, -1 - block).astype(F32)
    rank = jnp.sum((key.T > key).astype(F32), axis=1, keepdims=True).astype(jnp.int32)
    place = lax.broadcasted_iota(jnp.int32, (blocks, 128), 1)
    return jnp.sum(jnp.where(rank == place, key, 0.0), axis=0, keepdims=True).astype(jnp.int32)


class Sizes:
    def __init__(self, mesh_shape, slots, pairs):
        self.rows, self.cols, self.reps = mesh_shape["row"], mesh_shape["col"], mesh_shape["rep"]
        self.slots, self.pairs = slots, pairs
        self.tile = self.reps * slots
        self.panel = self.cols * self.tile
        self.tiles = self.rows * self.cols
        self.blocks = self.tiles * self.tile
        self.half = self.tiles * slots
        self.strip = self.cols * slots


def pack_kernel(sizes, density, left_index, right_index, pair_count, out, blocks, lefts, rights, counts, sems):
    copies = [
        pltpu.make_async_copy(source, target, sems.at[i])
        for i, (source, target) in enumerate(
            ((density, blocks), (left_index, lefts), (right_index, rights), (pair_count, counts))
        )
    ]
    for copy in copies:
        copy.start()
    row, col = lax.axis_index("row"), lax.axis_index("col")
    for copy in copies[1:]:
        copy.wait()
    position = lax.broadcasted_iota(jnp.int32, (sizes.slots, sizes.pairs), 1)
    slot = lax.broadcasted_iota(jnp.int32, (sizes.slots, sizes.pairs), 0)
    codes = []
    for n in range(STEPS):
        for q in range(2):
            live = jnp.zeros((sizes.slots, sizes.pairs), jnp.int32)
            for s in range(sizes.slots):
                live = jnp.where(slot == s, counts[n, q, s], live)
            right = rights[n, q]
            inside = lax.rem(right, sizes.tile)
            left = lefts[n, q] + (row * sizes.panel if n == 0 else 0)
            right = (right - inside) * sizes.cols + col * sizes.tile + inside
            dead = position >= live
            left = jnp.where(dead, sizes.blocks if n == 0 else sizes.panel, left)
            right = jnp.where(dead, sizes.blocks, right)
            codes.append(((live * CODE + left) * CODE + right).astype(F32))
    out[sizes.slots * 32 : sizes.slots * 33] = jnp.concatenate(codes, axis=1)
    copies[0].wait()
    for s in range(sizes.slots):
        out[s * 32 : s * 32 + 32] = jnp.concatenate([blocks[s, :32], blocks[s, 32:]], axis=1)


def first_square_kernel(sizes, offsets, *refs):
    pieces, refs = refs[: len(offsets)], refs[len(offsets) :]
    out, right_ref, codes_out, left_ref, codes, sem, payload, payload_sem = refs
    row, col, rep = lax.axis_index("row"), lax.axis_index("col"), lax.axis_index("rep")
    fetch = pltpu.make_async_copy(pieces[-1], payload, payload_sem)
    fetch.start()
    pieces = pieces[:-1] + (payload,)

    def unpack(piece, offset):
        m, n, e = offset
        tile = (row ^ m) * sizes.cols + (col ^ n)
        base = pl.multiple_of(tile * sizes.tile + (rep ^ e) * sizes.slots, sizes.slots)
        for s in range(sizes.slots):
            twice = spread(piece[s * 32 : s * 32 + 32])
            store_left(left_ref, base + s, twice)
            store_right(right_ref, base + s, twice)

    def unpack_codes(piece, offset):
        m, n, e = offset
        if e == 0:
            place = pl.multiple_of(((row ^ m) * sizes.cols + (col ^ n)) * sizes.slots, sizes.slots)
            codes_out[pl.ds(place, sizes.slots)] = piece[sizes.slots * 32 : sizes.slots * 33].astype(jnp.int32)

    fetch.wait()
    for piece, offset in zip(pieces, offsets):
        unpack_codes(piece, offset)
    mine = lambda place: place < sizes.half
    wanted = (mine, mine, lambda place: mine(place) & (place // sizes.strip == row))
    for product, choice in enumerate(wanted):
        order = order_by_count(codes_out[: sizes.blocks], product * sizes.pairs, choice, sizes.blocks)
        codes_out[sizes.half + product : sizes.half + product + 1] = order
    copy = pltpu.make_async_copy(codes_out.at[pl.ds(0, sizes.half + 8)], codes, sem)
    copy.start()
    zero_block(left_ref, sizes.blocks, right_ref, sizes.blocks)
    for piece, offset in zip(pieces, offsets):
        unpack(piece, offset)
    copy.wait()

    def finish(place, twice):
        out[place] = pack(twice)

    ordered_products(sizes, codes, sizes.half, 0, 0, sizes.half, 16, left_ref, right_ref, finish)


def first_cube_kernel(sizes, own, other, right_ref, codes_in, out, left_ref, codes, sem):
    copy = pltpu.make_async_copy(codes_in.at[pl.ds(0, sizes.half + 8)], codes, sem)
    copy.start()
    rep = lax.axis_index("rep")
    zero_block(left_ref, sizes.blocks, None, None)

    def prepare_tile(i, carry):
        for e, source in ((rep, own), (1 - rep, other)):
            for s in range(sizes.slots):
                store_left(
                    left_ref, (i * sizes.reps + e) * sizes.slots + s, spread(source[i * sizes.slots + s])
                )
        return carry

    lax.fori_loop(0, sizes.tiles, prepare_tile, 0)
    copy.wait()

    def finish(place, twice):
        out[place] = 3.0 * own[place] - 2.0 * pack(twice)

    ordered_products(sizes, codes, sizes.half, 0, 1, sizes.half, 16, left_ref, right_ref, finish)


def last_square_kernel(sizes, own, other, codes_in, out, right_ref, left_ref, codes, sems):
    row, rep = lax.axis_index("row"), lax.axis_index("rep")
    first = pl.multiple_of(row * sizes.strip, sizes.strip)
    copies = [
        pltpu.make_async_copy(codes_in.at[pl.ds(first, sizes.strip)], codes.at[pl.ds(0, sizes.strip)], sems.at[0]),
        pltpu.make_async_copy(codes_in.at[pl.ds(sizes.half, 8)], codes.at[pl.ds(sizes.strip, 8)], sems.at[1]),
    ]
    for copy in copies:
        copy.start()
    zero_block(left_ref, sizes.panel, right_ref, sizes.blocks)

    def prepare_tile(i, carry):
        for e, source in ((rep, own), (1 - rep, other)):
            for s in range(sizes.slots):
                store_right(
                    right_ref, (i * sizes.reps + e) * sizes.slots + s, spread(source[i * sizes.slots + s])
                )
        return carry

    lax.fori_loop(0, sizes.tiles, prepare_tile, 0)
    for n in range(sizes.cols):
        for e, source in ((rep, own), (1 - rep, other)):
            for s in range(sizes.slots):
                twice = spread(source[(row * sizes.cols + n) * sizes.slots + s])
                store_left(left_ref, (n * sizes.reps + e) * sizes.slots + s, twice)
    for copy in copies:
        copy.wait()

    def finish(place, twice):
        out[place] = pack(twice)

    ordered_products(sizes, codes, sizes.strip, first, 2, sizes.strip, 8, left_ref, right_ref, finish)


def last_cube_kernel(sizes, own, other, right_ref, codes_in, out, left_ref, codes, sem):
    row, col, rep = lax.axis_index("row"), lax.axis_index("col"), lax.axis_index("rep")
    base = pl.multiple_of((row * sizes.cols + col) * sizes.slots, sizes.slots)
    copy = pltpu.make_async_copy(codes_in.at[pl.ds(base, sizes.slots)], codes, sem)
    copy.start()
    zero_block(left_ref, sizes.panel, None, None)
    for n in range(sizes.cols):
        for e, source in ((rep, own), (1 - rep, other)):
            for s in range(sizes.slots):
                twice = spread(source[n * sizes.slots + s])
                store_left(left_ref, (n * sizes.reps + e) * sizes.slots + s, twice)
    copy.wait()
    for s in range(sizes.slots):
        cube = fold(block_products(codes, s, 3 * sizes.pairs, sizes.pairs, left_ref, right_ref))
        square = spread(own[col * sizes.slots + s])
        out[s] = (3.0 * square - 2.0 * cube)[:, :64]


def call(kernel, sizes, outs, in_specs, out_specs, scratch, limit=40):
    return pl.pallas_call(
        functools.partial(kernel, sizes),
        out_shape=outs,
        in_specs=in_specs,
        out_specs=out_specs,
        scratch_shapes=scratch,
        compiler_params=pltpu.CompilerParams(vmem_limit_bytes=limit * 2**20),
    )


def whole_form(sizes, density, left_index, right_index, pair_count):
    width = density.shape[1]
    index_shape = (STEPS, 2, sizes.slots, sizes.pairs)
    code_shape = (sizes.blocks + 8, STEPS * 2 * sizes.pairs)
    packed = lambda count: jax.ShapeDtypeStruct((count, 32, 128), F32)
    rights = jax.ShapeDtypeStruct((sizes.blocks + 1, 64, 128), BF16)
    code_scratch = [
        pltpu.SMEM((sizes.half + 8, code_shape[1]), jnp.int32),
        pltpu.SemaphoreType.DMA,
    ]

    payload = call(
        pack_kernel,
        sizes,
        jax.ShapeDtypeStruct((sizes.slots * 33, 128), F32),
        [ANY] * 4,
        VMEM,
        [
            pltpu.VMEM((sizes.slots, width, width), F32),
            pltpu.VMEM(index_shape, jnp.int32),
            pltpu.VMEM(index_shape, jnp.int32),
            pltpu.SMEM((STEPS, 2, sizes.slots), jnp.int32),
            pltpu.SemaphoreType.DMA((4,)),
        ],
        limit=62,
    )(density, left_index, right_index, pair_count)

    def swap(value, axes, mask, size):
        return lax.ppermute(value, axes, [(i, i ^ mask) for i in range(size)])

    def row_swap(value, m):
        return swap(value, "row", m, 4)

    def col_swap(value):
        return swap(value, "col", 1, 2)

    def rep_swap(value):
        return swap(value, "rep", 1, 2)

    far, near, across = row_swap(payload, 2), row_swap(payload, 1), col_swap(payload)
    near_across, farthest = col_swap(near), row_swap(far, 1)
    far_across, farthest_across = col_swap(far), swap(far, ("row", "col"), 3, 8)
    own = [
        ((0, 0, 0), swap(payload, "rep", 0, 2)),
        ((1, 0, 0), near),
        ((1, 1, 0), near_across),
        ((0, 1, 0), across),
        ((2, 0, 0), far),
        ((3, 0, 0), farthest),
        ((2, 1, 0), far_across),
        ((3, 1, 0), farthest_across),
    ]
    pieces = [pair for (m, n, e), piece in own for pair in (((m, n, e), piece), ((m, n, 1), rep_swap(piece)))]
    offsets, pieces = zip(*pieces[::-1])

    square, right, codes = call(
        lambda *args: first_square_kernel(args[0], offsets, *args[1:]),
        sizes,
        [packed(sizes.half), rights, jax.ShapeDtypeStruct(code_shape, jnp.int32)],
        [VMEM] * (len(pieces) - 1) + [ANY],
        [VMEM] * 3,
        [pltpu.VMEM((sizes.blocks + 1, 128, 128), BF16)]
        + code_scratch
        + [pltpu.VMEM(payload.shape, F32), pltpu.SemaphoreType.DMA],
    )(*pieces)
    current = call(
        first_cube_kernel,
        sizes,
        packed(sizes.half),
        [VMEM] * 3 + [ANY],
        VMEM,
        [pltpu.VMEM((sizes.blocks + 1, 128, 128), BF16)] + code_scratch,
    )(square, rep_swap(square), right, codes)
    square, right = call(
        last_square_kernel,
        sizes,
        [packed(sizes.cols * sizes.slots), rights],
        [VMEM] * 2 + [ANY],
        [VMEM] * 2,
        [
            pltpu.VMEM((sizes.panel + 1, 128, 128), BF16),
            pltpu.SMEM((sizes.strip + 8, code_shape[1]), jnp.int32),
            pltpu.SemaphoreType.DMA((2,)),
        ],
    )(current, rep_swap(current), codes)
    return call(
        last_cube_kernel,
        sizes,
        jax.ShapeDtypeStruct(density.shape, F32),
        [VMEM] * 3 + [ANY],
        VMEM,
        [
            pltpu.VMEM((sizes.panel + 1, 128, 128), BF16),
            pltpu.SMEM((sizes.slots, code_shape[1]), jnp.int32),
            pltpu.SemaphoreType.DMA,
        ],
    )(square, rep_swap(square), right, codes)


def solution(mesh):
    def local(density, left_index, right_index, pair_count):
        sizes = Sizes(mesh.shape, density.shape[0], left_index.shape[3])
        fits = (
            (sizes.rows, sizes.cols, sizes.reps, sizes.slots, sizes.pairs) == (4, 2, 2, 8, 32)
            and density.shape[1:] == (64, 64)
        )
        if fits:
            return whole_form(sizes, density, left_index, right_index, pair_count)
        return panel_form(density, left_index, right_index, pair_count)

    in_specs = (
        P(("groups", "row", "col", "rep"), None, None),
        P(None, None, ("groups", "row", "col", "rep"), None),
        P(None, None, ("groups", "row", "col", "rep"), None),
        P(None, None, ("groups", "row", "col", "rep")),
    )
    out_specs = P(("groups", "row", "col", "rep"), None, None)
    return jax.shard_map(local, mesh=mesh, in_specs=in_specs, out_specs=out_specs, check_vma=False)
```

```python
import functools

import jax
import jax.numpy as jnp
from jax import lax
from jax.experimental import pallas as pl
from jax.experimental.pallas import tpu as pltpu
from jax.sharding import PartitionSpec as P

STEPS = 2
CODE = 256
CHUNK = 4
VMEM = pl.BlockSpec(memory_space=pltpu.VMEM)
ANY = pl.BlockSpec(memory_space=pl.ANY)
BF16 = jnp.bfloat16
F32 = jnp.float32


def middle_view(blocks):
    width = blocks.shape[1]
    padded = jnp.concatenate([blocks, jnp.zeros((1, width, width), blocks.dtype)], axis=0)
    return jnp.transpose(padded, (1, 0, 2))


def multiply(left_blocks, right_blocks, left_rows, right_rows, live_counts):
    slot_count, pair_width = left_rows.shape
    width = left_blocks.shape[1]
    left_view = middle_view(left_blocks)
    right_view = middle_view(right_blocks)
    positions = jnp.arange(pair_width, dtype=jnp.int32)
    live = positions[None, :] < live_counts[:, None]
    left_pick = jnp.where(live, left_rows, left_blocks.shape[0]).reshape(slot_count * pair_width)
    right_pick = jnp.where(live, right_rows, right_blocks.shape[0]).reshape(slot_count * pair_width)
    left_taken = jnp.take(left_view, left_pick, axis=1).reshape(
        width, slot_count, pair_width, width
    )
    right_taken = jnp.take(right_view, right_pick, axis=1).reshape(
        width, slot_count, pair_width, width
    )
    return jnp.einsum("iskj,jskl->sil", left_taken, right_taken, precision=lax.Precision.HIGHEST)


def panel_form(density, left_index, right_index, pair_count):
    current = density
    for step in range(STEPS):
        row_blocks = lax.all_gather(current, ("col", "rep"), axis=0, tiled=True)
        column_blocks = lax.all_gather(current, ("row", "rep"), axis=0, tiled=True)
        square = multiply(
            row_blocks,
            column_blocks,
            left_index[step, 0],
            right_index[step, 0],
            pair_count[step, 0],
        )
        square_rows = lax.all_gather(square, ("col", "rep"), axis=0, tiled=True)
        cube = multiply(
            square_rows,
            column_blocks,
            left_index[step, 1],
            right_index[step, 1],
            pair_count[step, 1],
        )
        current = 3.0 * square - 2.0 * cube
    return current


def left_lanes(rows):
    return lax.broadcasted_iota(jnp.int32, (rows, 128), 1) < 64


def spread(packed):
    turned = pltpu.roll(packed, 64, 1)
    left = left_lanes(32)
    return jnp.concatenate([jnp.where(left, packed, turned), jnp.where(left, turned, packed)], axis=0)


def pack(twice):
    return jnp.where(left_lanes(32), twice[:32], twice[32:])


def halves(twice):
    high = twice.astype(BF16)
    return high, twice - high.astype(F32)


def store_left(ref, at, twice):
    high, low = halves(twice)
    ref[at, 0:64] = high
    ref[at, 64:128] = low.astype(BF16)


def store_right(ref, at, twice):
    high, low = halves(twice)
    ref[at] = jnp.where(left_lanes(64), high.astype(F32), low).astype(BF16)


def prepare(source, first, count, base, left_ref, right_ref, unroll=8):
    def body(i, carry):
        twice = spread(source[first + i])
        if left_ref is not None:
            store_left(left_ref, base + i, twice)
        if right_ref is not None:
            store_right(right_ref, base + i, twice)
        return carry

    lax.fori_loop(0, count, body, 0, unroll=unroll)


def zero_block(left_ref, left_at, right_ref, right_at):
    if left_ref is not None:
        left_ref[left_at] = jnp.zeros((128, 128), BF16)
    if right_ref is not None:
        right_ref[right_at] = jnp.zeros((64, 128), BF16)


def block_products(codes, at, lane, pairs, left_ref, right_ref):
    mask = left_lanes(128)
    total = jnp.zeros((128, 128), F32)
    for start in range(0, pairs, CHUNK):
        lefts, rights = [], []
        for p in range(start, start + CHUNK):
            code = codes[at, lane + p]
            lefts.append(left_ref[(code >> 8) & (CODE - 1)])
            rights.append(right_ref[code & (CODE - 1)])
        left = jnp.concatenate(
            [jnp.where(mask, lefts[0], lefts[1]), jnp.where(mask, lefts[2], lefts[3])], axis=1
        )
        right = jnp.concatenate(rights, axis=0)
        total = total + jnp.dot(left, right, preferred_element_type=F32)
    return total


def fold(total):
    both = total[:64] + total[64:]
    return both + pltpu.roll(both, 64, 1)


def ordered_products(sizes, codes, line, first, product, blocks, group, left_ref, right_ref, finish):
    lane = product * sizes.pairs
    limits = (0, sizes.pairs // 2, 3 * sizes.pairs // 4, sizes.pairs)

    def body(g, carry):
        most = codes[line + product, g * group] >> 8
        for low, high in zip(limits[:-1], limits[1:]):

            @pl.when((most > low) & (most <= high))
            def _():
                for s in range(group):
                    place = (codes[line + product, g * group + s] & (CODE - 1)) - first
                    finish(place, fold(block_products(codes, place, lane, high, left_ref, right_ref)))

        return carry

    lax.fori_loop(0, blocks // group, body, 0)


def order_by_count(codes, lane, wanted, blocks):
    block = lax.broadcasted_iota(jnp.int32, (blocks, 128), 0)
    count = jnp.broadcast_to(codes[:, lane : lane + 1] >> 16, (blocks, 128))
    key = jnp.where(wanted(block), count * CODE + block, -1 - block).astype(F32)
    rank = jnp.sum((key.T > key).astype(F32), axis=1, keepdims=True).astype(jnp.int32)
    place = lax.broadcasted_iota(jnp.int32, (blocks, 128), 1)
    return jnp.sum(jnp.where(rank == place, key, 0.0), axis=0, keepdims=True).astype(jnp.int32)


class Sizes:
    def __init__(self, mesh_shape, slots, pairs):
        self.rows, self.cols, self.reps = mesh_shape["row"], mesh_shape["col"], mesh_shape["rep"]
        self.slots, self.pairs = slots, pairs
        self.tile = self.reps * slots
        self.panel = self.cols * self.tile
        self.tiles = self.rows * self.cols
        self.blocks = self.tiles * self.tile
        self.half = self.blocks // 2


def pack_kernel(sizes, density, left_index, right_index, pair_count, out, blocks, lefts, rights, counts, sems):
    copies = [
        pltpu.make_async_copy(source, target, sems.at[i])
        for i, (source, target) in enumerate(
            ((density, blocks), (left_index, lefts), (right_index, rights), (pair_count, counts))
        )
    ]
    for copy in copies:
        copy.start()
    row, col = lax.axis_index("row"), lax.axis_index("col")
    for copy in copies[1:]:
        copy.wait()
    position = lax.broadcasted_iota(jnp.int32, (sizes.slots, sizes.pairs), 1)
    slot = lax.broadcasted_iota(jnp.int32, (sizes.slots, sizes.pairs), 0)
    codes = []
    for n in range(STEPS):
        for q in range(2):
            live = jnp.zeros((sizes.slots, sizes.pairs), jnp.int32)
            for s in range(sizes.slots):
                live = jnp.where(slot == s, counts[n, q, s], live)
            right = rights[n, q]
            inside = lax.rem(right, sizes.tile)
            left = lefts[n, q] + (lax.rem(row, sizes.rows // 2) * sizes.panel if n == 0 else 0)
            right = (right - inside) * sizes.cols + col * sizes.tile + inside
            dead = position >= live
            left = jnp.where(dead, sizes.half if n == 0 else sizes.panel, left)
            right = jnp.where(dead, sizes.blocks, right)
            codes.append(((live * CODE + left) * CODE + right).astype(F32))
    out[sizes.slots * 32 : sizes.slots * 33] = jnp.concatenate(codes, axis=1)
    copies[0].wait()
    for s in range(sizes.slots):
        out[s * 32 : s * 32 + 32] = jnp.concatenate([blocks[s, :32], blocks[s, 32:]], axis=1)


def first_step_kernel(sizes, offsets, *refs):
    pieces, refs = refs[: len(offsets)], refs[len(offsets) :]
    out, codes_out, left_ref, right_ref, square_ref, squares, codes, sems = refs
    row, col, rep = lax.axis_index("row"), lax.axis_index("col"), lax.axis_index("rep")

    def place_of(offset):
        m, n, e = offset
        tile = (row ^ m) * sizes.cols + (col ^ n)
        return pl.multiple_of(tile * sizes.tile + (rep ^ e) * sizes.slots, sizes.slots)

    for piece, offset in zip(pieces, offsets):
        code = piece[sizes.slots * 32 : sizes.slots * 33].astype(jnp.int32)
        codes_out[pl.ds(place_of(offset), sizes.slots)] = code
    first = pl.multiple_of(rep * sizes.half, sizes.half)
    mine = lambda t: t // sizes.half == rep
    for product, wanted in enumerate((mine, mine, lambda t: t // sizes.panel == row)):
        order = order_by_count(codes_out[: sizes.blocks], product * sizes.pairs, wanted, sizes.blocks)
        codes_out[sizes.blocks + product : sizes.blocks + product + 1] = order
    copies = [
        pltpu.make_async_copy(codes_out.at[pl.ds(first, sizes.half)], codes.at[pl.ds(0, sizes.half)], sems.at[0]),
        pltpu.make_async_copy(codes_out.at[pl.ds(sizes.blocks, 8)], codes.at[pl.ds(sizes.half, 8)], sems.at[1]),
    ]
    for copy in copies:
        copy.start()

    zero_block(left_ref, sizes.half, right_ref, sizes.blocks)
    zero_block(square_ref, sizes.half, None, None)
    for piece, offset in zip(pieces, offsets):
        base = place_of(offset)
        for s in range(sizes.slots):
            store_right(right_ref, base + s, spread(piece[s * 32 : s * 32 + 32]))
    for far in range(2):

        @pl.when(row // (sizes.rows // 2) ^ far == rep)
        def _():
            for piece, offset in zip(pieces, offsets):
                if offset[0] // (sizes.rows // 2) == far:
                    base = place_of(offset) - first
                    for s in range(sizes.slots):
                        store_left(left_ref, base + s, spread(piece[s * 32 : s * 32 + 32]))

    for copy in copies:
        copy.wait()

    def finish_square(place, twice):
        store_left(square_ref, place, twice)
        squares[place] = pack(twice)

    def finish_cube(place, twice):
        out[place] = 3.0 * squares[place] - 2.0 * pack(twice)

    ordered_products(sizes, codes, sizes.half, first, 0, sizes.half, 16, left_ref, right_ref, finish_square)
    ordered_products(sizes, codes, sizes.half, first, 1, sizes.half, 16, square_ref, right_ref, finish_cube)


def last_step_kernel(sizes, own, other, codes_in, out, left_ref, right_ref, square_ref, squares, codes, sems):
    row, col, rep = lax.axis_index("row"), lax.axis_index("col"), lax.axis_index("rep")
    first = pl.multiple_of(row * sizes.panel, sizes.panel)
    copies = [
        pltpu.make_async_copy(codes_in.at[pl.ds(first, sizes.panel)], codes.at[pl.ds(0, sizes.panel)], sems.at[0]),
        pltpu.make_async_copy(codes_in.at[pl.ds(sizes.blocks, 8)], codes.at[pl.ds(sizes.panel, 8)], sems.at[1]),
    ]
    for copy in copies:
        copy.start()
    zero_block(left_ref, sizes.panel, right_ref, sizes.blocks)
    zero_block(square_ref, sizes.panel, None, None)
    unroll = 2 * sizes.slots
    for part, source in ((rep, own), (1 - rep, other)):

        def prepare_right(i, carry):
            for s in range(unroll):
                at = i * unroll + s
                store_right(right_ref, part * sizes.half + at, spread(source[at]))
            return carry

        lax.fori_loop(0, sizes.half // unroll, prepare_right, 0)

        @pl.when(row // (sizes.rows // 2) == part)
        def _():
            base = lax.rem(row, sizes.rows // 2) * sizes.panel
            for s in range(sizes.panel):
                store_left(left_ref, s, spread(source[base + s]))

    for copy in copies:
        copy.wait()

    def finish_square(place, twice):
        store_left(square_ref, place, twice)
        squares[place] = pack(twice)

    ordered_products(sizes, codes, sizes.panel, first, 2, sizes.panel, 16, left_ref, right_ref, finish_square)
    base = (col * sizes.reps + rep) * sizes.slots
    for s in range(sizes.slots):
        cube = fold(block_products(codes, base + s, 3 * sizes.pairs, sizes.pairs, square_ref, right_ref))
        out[s] = (3.0 * spread(squares[base + s]) - 2.0 * cube)[:, :64]


def call(kernel, sizes, outs, in_specs, out_specs, scratch, limit=40):
    return pl.pallas_call(
        functools.partial(kernel, sizes),
        out_shape=outs,
        in_specs=in_specs,
        out_specs=out_specs,
        scratch_shapes=scratch,
        compiler_params=pltpu.CompilerParams(vmem_limit_bytes=limit * 2**20),
    )


def whole_form(sizes, density, left_index, right_index, pair_count):
    width = density.shape[1]
    index_shape = (STEPS, 2, sizes.slots, sizes.pairs)
    code_shape = (sizes.blocks + 8, STEPS * 2 * sizes.pairs)
    packed = jax.ShapeDtypeStruct((sizes.half, 32, 128), F32)

    def scratch(blocks):
        return [
            pltpu.VMEM((blocks + 1, 128, 128), BF16),
            pltpu.VMEM((sizes.blocks + 1, 64, 128), BF16),
            pltpu.VMEM((blocks + 1, 128, 128), BF16),
            pltpu.VMEM((blocks, 32, 128), F32),
            pltpu.SMEM((blocks + 8, code_shape[1]), jnp.int32),
            pltpu.SemaphoreType.DMA((2,)),
        ]

    payload = call(
        pack_kernel,
        sizes,
        jax.ShapeDtypeStruct((sizes.slots * 33, 128), F32),
        [ANY] * 4,
        VMEM,
        [
            pltpu.VMEM((sizes.slots, width, width), F32),
            pltpu.VMEM(index_shape, jnp.int32),
            pltpu.VMEM(index_shape, jnp.int32),
            pltpu.SMEM((STEPS, 2, sizes.slots), jnp.int32),
            pltpu.SemaphoreType.DMA((4,)),
        ],
        limit=62,
    )(density, left_index, right_index, pair_count)

    def swap(value, axes, mask, size):
        return lax.ppermute(value, axes, [(i, i ^ mask) for i in range(size)])

    def row_swap(value, m):
        return swap(value, "row", m, 4)

    def col_swap(value):
        return swap(value, "col", 1, 2)

    def rep_swap(value):
        return swap(value, "rep", 1, 2)

    far, near, across = row_swap(payload, 2), row_swap(payload, 1), col_swap(payload)
    near_across, farthest = col_swap(near), row_swap(far, 1)
    far_across, farthest_across = col_swap(far), swap(far, ("row", "col"), 3, 8)
    own = [
        ((0, 0, 0), swap(payload, "rep", 0, 2)),
        ((1, 0, 0), near),
        ((1, 1, 0), near_across),
        ((0, 1, 0), across),
        ((2, 0, 0), far),
        ((3, 0, 0), farthest),
        ((2, 1, 0), far_across),
        ((3, 1, 0), farthest_across),
    ]
    pieces = [pair for (m, n, e), piece in own for pair in (((m, n, e), piece), ((m, n, 1), rep_swap(piece)))]
    offsets, pieces = zip(*pieces[::-1])
    current, codes = call(
        lambda *args: first_step_kernel(args[0], offsets, *args[1:]),
        sizes,
        [packed, jax.ShapeDtypeStruct(code_shape, jnp.int32)],
        [VMEM] * len(pieces),
        [VMEM] * 2,
        scratch(sizes.half),
    )(*pieces)
    return call(
        last_step_kernel,
        sizes,
        jax.ShapeDtypeStruct(density.shape, F32),
        [VMEM] * 2 + [ANY],
        VMEM,
        scratch(sizes.panel),
    )(current, rep_swap(current), codes)


def solution(mesh):
    def local(density, left_index, right_index, pair_count):
        sizes = Sizes(mesh.shape, density.shape[0], left_index.shape[3])
        fits = (
            (sizes.rows, sizes.cols, sizes.reps, sizes.slots, sizes.pairs) == (4, 2, 2, 8, 32)
            and density.shape[1:] == (64, 64)
        )
        if fits:
            return whole_form(sizes, density, left_index, right_index, pair_count)
        return panel_form(density, left_index, right_index, pair_count)

    in_specs = (
        P(("groups", "row", "col", "rep"), None, None),
        P(None, None, ("groups", "row", "col", "rep"), None),
        P(None, None, ("groups", "row", "col", "rep"), None),
        P(None, None, ("groups", "row", "col", "rep")),
    )
    out_specs = P(("groups", "row", "col", "rep"), None, None)
    return jax.shard_map(local, mesh=mesh, in_specs=in_specs, out_specs=out_specs, check_vma=False)
```

```python
import functools

import jax
import jax.numpy as jnp
from jax import lax
from jax.experimental import pallas as pl
from jax.experimental.pallas import tpu as pltpu
from jax.sharding import PartitionSpec as P

STEPS = 2
CODE = 256
CHUNK = 4
VMEM = pl.BlockSpec(memory_space=pltpu.VMEM)
ANY = pl.BlockSpec(memory_space=pl.ANY)
BF16 = jnp.bfloat16
F32 = jnp.float32


def middle_view(blocks):
    width = blocks.shape[1]
    padded = jnp.concatenate([blocks, jnp.zeros((1, width, width), blocks.dtype)], axis=0)
    return jnp.transpose(padded, (1, 0, 2))


def multiply(left_blocks, right_blocks, left_rows, right_rows, live_counts):
    slot_count, pair_width = left_rows.shape
    width = left_blocks.shape[1]
    left_view = middle_view(left_blocks)
    right_view = middle_view(right_blocks)
    positions = jnp.arange(pair_width, dtype=jnp.int32)
    live = positions[None, :] < live_counts[:, None]
    left_pick = jnp.where(live, left_rows, left_blocks.shape[0]).reshape(slot_count * pair_width)
    right_pick = jnp.where(live, right_rows, right_blocks.shape[0]).reshape(slot_count * pair_width)
    left_taken = jnp.take(left_view, left_pick, axis=1).reshape(
        width, slot_count, pair_width, width
    )
    right_taken = jnp.take(right_view, right_pick, axis=1).reshape(
        width, slot_count, pair_width, width
    )
    return jnp.einsum("iskj,jskl->sil", left_taken, right_taken, precision=lax.Precision.HIGHEST)


def panel_form(density, left_index, right_index, pair_count):
    current = density
    for step in range(STEPS):
        row_blocks = lax.all_gather(current, ("col", "rep"), axis=0, tiled=True)
        column_blocks = lax.all_gather(current, ("row", "rep"), axis=0, tiled=True)
        square = multiply(
            row_blocks,
            column_blocks,
            left_index[step, 0],
            right_index[step, 0],
            pair_count[step, 0],
        )
        square_rows = lax.all_gather(square, ("col", "rep"), axis=0, tiled=True)
        cube = multiply(
            square_rows,
            column_blocks,
            left_index[step, 1],
            right_index[step, 1],
            pair_count[step, 1],
        )
        current = 3.0 * square - 2.0 * cube
    return current


def left_lanes(rows):
    return lax.broadcasted_iota(jnp.int32, (rows, 128), 1) < 64


def spread(packed):
    turned = pltpu.roll(packed, 64, 1)
    left = left_lanes(32)
    return jnp.concatenate([jnp.where(left, packed, turned), jnp.where(left, turned, packed)], axis=0)


def pack(twice):
    return jnp.where(left_lanes(32), twice[:32], twice[32:])


def halves(twice):
    high = twice.astype(BF16)
    return high, twice - high.astype(F32)


def store_left(ref, at, twice):
    high, low = halves(twice)
    ref[at, 0:64] = high
    ref[at, 64:128] = low.astype(BF16)


def store_right(ref, at, twice):
    high, low = halves(twice)
    ref[at] = jnp.where(left_lanes(64), high.astype(F32), low).astype(BF16)


def zero_block(left_ref, left_at, right_ref, right_at):
    if left_ref is not None:
        left_ref[left_at] = jnp.zeros((128, 128), BF16)
    if right_ref is not None:
        right_ref[right_at] = jnp.zeros((64, 128), BF16)


def block_products(codes, places, lane, pairs, left_ref, right_ref):
    mask = left_lanes(128)
    totals = [jnp.zeros((128, 128), F32) for _ in places]
    for start in range(0, pairs, CHUNK):
        for i, place in enumerate(places):
            lefts, rights = [], []
            for p in range(start, start + CHUNK):
                code = codes[place, lane + p]
                lefts.append(left_ref[(code >> 8) & (CODE - 1)])
                rights.append(right_ref[code & (CODE - 1)])
            left = jnp.concatenate(
                [jnp.where(mask, lefts[0], lefts[1]), jnp.where(mask, lefts[2], lefts[3])], axis=1
            )
            right = jnp.concatenate(rights, axis=0)
            totals[i] = totals[i] + jnp.dot(left, right, preferred_element_type=F32)
    return [total[:64] + total[64:] for total in totals]


def fold(both):
    return both + pltpu.roll(both, 64, 1)


def ordered_products(sizes, codes, line, first, product, blocks, left_ref, right_ref, sums, group=16):
    lane = product * sizes.pairs
    limits = (0, sizes.pairs // 2, 3 * sizes.pairs // 4, sizes.pairs)

    def body(g, carry):
        most = codes[line + product, g * group] >> 8
        for low, high in zip(limits[:-1], limits[1:]):

            @pl.when((most > low) & (most <= high))
            def _():
                for s in range(0, group, 2):
                    places = [(codes[line + product, g * group + s + i] & (CODE - 1)) - first for i in range(2)]
                    totals = block_products(codes, places, lane, high, left_ref, right_ref)
                    for place, total in zip(places, totals):
                        sums[place] = total

        return carry

    lax.fori_loop(0, blocks // group, body, 0)


def each(count, body, unroll=32):
    def step(i, carry):
        for s in range(unroll):
            body(i * unroll + s)
        return carry

    lax.fori_loop(0, count // unroll, step, 0)


def order_by_count(codes, lane, wanted, blocks):
    block = lax.broadcasted_iota(jnp.int32, (blocks, 128), 0)
    count = jnp.broadcast_to(codes[:, lane : lane + 1] >> 16, (blocks, 128))
    key = jnp.where(wanted(block), count * CODE + block, -1 - block).astype(F32)
    rank = jnp.sum((key.T > key).astype(F32), axis=1, keepdims=True).astype(jnp.int32)
    place = lax.broadcasted_iota(jnp.int32, (blocks, 128), 1)
    return jnp.sum(jnp.where(rank == place, key, 0.0), axis=0, keepdims=True).astype(jnp.int32)


class Sizes:
    def __init__(self, mesh_shape, slots, pairs):
        self.rows, self.cols, self.reps = mesh_shape["row"], mesh_shape["col"], mesh_shape["rep"]
        self.slots, self.pairs = slots, pairs
        self.tile = self.reps * slots
        self.panel = self.cols * self.tile
        self.tiles = self.rows * self.cols
        self.blocks = self.tiles * self.tile
        self.half = self.blocks // 2


def pack_kernel(sizes, density, left_index, right_index, pair_count, out, blocks, lefts, rights, counts, sems):
    copies = [
        pltpu.make_async_copy(source, target, sems.at[i])
        for i, (source, target) in enumerate(
            ((density, blocks), (left_index, lefts), (right_index, rights), (pair_count, counts))
        )
    ]
    for copy in copies:
        copy.start()
    row, col = lax.axis_index("row"), lax.axis_index("col")
    for copy in copies[1:]:
        copy.wait()
    position = lax.broadcasted_iota(jnp.int32, (sizes.slots, sizes.pairs), 1)
    slot = lax.broadcasted_iota(jnp.int32, (sizes.slots, sizes.pairs), 0)
    codes = []
    for n in range(STEPS):
        for q in range(2):
            live = jnp.zeros((sizes.slots, sizes.pairs), jnp.int32)
            for s in range(sizes.slots):
                live = jnp.where(slot == s, counts[n, q, s], live)
            right = rights[n, q]
            inside = lax.rem(right, sizes.tile)
            left = lefts[n, q] + (lax.rem(row, sizes.rows // 2) * sizes.panel if n == 0 else 0)
            right = (right - inside) * sizes.cols + col * sizes.tile + inside
            dead = position >= live
            left = jnp.where(dead, sizes.half if n == 0 else sizes.panel, left)
            right = jnp.where(dead, sizes.blocks, right)
            codes.append(((live * CODE + left) * CODE + right).astype(F32))
    out[sizes.slots * 32 : sizes.slots * 33] = jnp.concatenate(codes, axis=1)
    copies[0].wait()
    for s in range(sizes.slots):
        out[s * 32 : s * 32 + 32] = jnp.concatenate([blocks[s, :32], blocks[s, 32:]], axis=1)


def first_step_kernel(sizes, offsets, *refs):
    pieces, refs = refs[: len(offsets)], refs[len(offsets) :]
    out, codes_out, left_ref, right_ref, square_ref, squares, sums, codes, sems = refs
    row, col, rep = lax.axis_index("row"), lax.axis_index("col"), lax.axis_index("rep")

    def place_of(offset):
        m, n, e = offset
        tile = (row ^ m) * sizes.cols + (col ^ n)
        return pl.multiple_of(tile * sizes.tile + (rep ^ e) * sizes.slots, sizes.slots)

    for piece, offset in zip(pieces, offsets):
        code = piece[sizes.slots * 32 : sizes.slots * 33].astype(jnp.int32)
        codes_out[pl.ds(place_of(offset), sizes.slots)] = code
    first = pl.multiple_of(rep * sizes.half, sizes.half)
    mine = lambda t: t // sizes.half == rep
    for product, wanted in enumerate((mine, mine, lambda t: t // sizes.panel == row)):
        order = order_by_count(codes_out[: sizes.blocks], product * sizes.pairs, wanted, sizes.blocks)
        codes_out[sizes.blocks + product : sizes.blocks + product + 1] = order
    copies = [
        pltpu.make_async_copy(codes_out.at[pl.ds(first, sizes.half)], codes.at[pl.ds(0, sizes.half)], sems.at[0]),
        pltpu.make_async_copy(codes_out.at[pl.ds(sizes.blocks, 8)], codes.at[pl.ds(sizes.half, 8)], sems.at[1]),
    ]
    for copy in copies:
        copy.start()

    zero_block(left_ref, sizes.half, right_ref, sizes.blocks)
    zero_block(square_ref, sizes.half, None, None)
    for piece, offset in zip(pieces, offsets):
        base = place_of(offset)
        for s in range(sizes.slots):
            store_right(right_ref, base + s, spread(piece[s * 32 : s * 32 + 32]))
    for far in range(2):

        @pl.when(row // (sizes.rows // 2) ^ far == rep)
        def _():
            for piece, offset in zip(pieces, offsets):
                if offset[0] // (sizes.rows // 2) == far:
                    base = place_of(offset) - first
                    for s in range(sizes.slots):
                        store_left(left_ref, base + s, spread(piece[s * 32 : s * 32 + 32]))

    for copy in copies:
        copy.wait()

    def finish_square(place):
        twice = fold(sums[place])
        store_left(square_ref, place, twice)
        squares[place] = pack(twice)

    def finish_cube(place):
        out[place] = 3.0 * squares[place] - 2.0 * pack(fold(sums[place]))

    ordered_products(sizes, codes, sizes.half, first, 0, sizes.half, left_ref, right_ref, sums)
    each(sizes.half, finish_square)
    ordered_products(sizes, codes, sizes.half, first, 1, sizes.half, square_ref, right_ref, sums)
    each(sizes.half, finish_cube)


def last_step_kernel(sizes, own, other, codes_in, out, left_ref, right_ref, square_ref, squares, sums, codes, sems):
    row, col, rep = lax.axis_index("row"), lax.axis_index("col"), lax.axis_index("rep")
    first = pl.multiple_of(row * sizes.panel, sizes.panel)
    copies = [
        pltpu.make_async_copy(codes_in.at[pl.ds(first, sizes.panel)], codes.at[pl.ds(0, sizes.panel)], sems.at[0]),
        pltpu.make_async_copy(codes_in.at[pl.ds(sizes.blocks, 8)], codes.at[pl.ds(sizes.panel, 8)], sems.at[1]),
    ]
    for copy in copies:
        copy.start()
    zero_block(left_ref, sizes.panel, right_ref, sizes.blocks)
    zero_block(square_ref, sizes.panel, None, None)
    for part, source in ((rep, own), (1 - rep, other)):

        def prepare_right(at):
            store_right(right_ref, part * sizes.half + at, spread(source[at]))

        each(sizes.half, prepare_right)

        @pl.when(row // (sizes.rows // 2) == part)
        def _():
            base = lax.rem(row, sizes.rows // 2) * sizes.panel
            for s in range(sizes.panel):
                store_left(left_ref, s, spread(source[base + s]))

    for copy in copies:
        copy.wait()

    def finish_square(place):
        twice = fold(sums[place])
        store_left(square_ref, place, twice)
        squares[place] = pack(twice)

    ordered_products(sizes, codes, sizes.panel, first, 2, sizes.panel, left_ref, right_ref, sums)
    each(sizes.panel, finish_square)
    base = (col * sizes.reps + rep) * sizes.slots
    for s in range(0, sizes.slots, 2):
        places = [base + s, base + s + 1]
        totals = block_products(codes, places, 3 * sizes.pairs, sizes.pairs, square_ref, right_ref)
        for i, place in enumerate(places):
            out[s + i] = (3.0 * spread(squares[place]) - 2.0 * fold(totals[i]))[:, :64]


def call(kernel, sizes, outs, in_specs, out_specs, scratch, limit=40):
    return pl.pallas_call(
        functools.partial(kernel, sizes),
        out_shape=outs,
        in_specs=in_specs,
        out_specs=out_specs,
        scratch_shapes=scratch,
        compiler_params=pltpu.CompilerParams(vmem_limit_bytes=limit * 2**20),
    )


def whole_form(sizes, density, left_index, right_index, pair_count):
    width = density.shape[1]
    index_shape = (STEPS, 2, sizes.slots, sizes.pairs)
    code_shape = (sizes.blocks + 8, STEPS * 2 * sizes.pairs)
    packed = jax.ShapeDtypeStruct((sizes.half, 32, 128), F32)

    def scratch(blocks):
        return [
            pltpu.VMEM((blocks + 1, 128, 128), BF16),
            pltpu.VMEM((sizes.blocks + 1, 64, 128), BF16),
            pltpu.VMEM((blocks + 1, 128, 128), BF16),
            pltpu.VMEM((blocks, 32, 128), F32),
            pltpu.VMEM((blocks, 64, 128), F32),
            pltpu.SMEM((blocks + 8, code_shape[1]), jnp.int32),
            pltpu.SemaphoreType.DMA((2,)),
        ]

    payload = call(
        pack_kernel,
        sizes,
        jax.ShapeDtypeStruct((sizes.slots * 33, 128), F32),
        [ANY] * 4,
        VMEM,
        [
            pltpu.VMEM((sizes.slots, width, width), F32),
            pltpu.VMEM(index_shape, jnp.int32),
            pltpu.VMEM(index_shape, jnp.int32),
            pltpu.SMEM((STEPS, 2, sizes.slots), jnp.int32),
            pltpu.SemaphoreType.DMA((4,)),
        ],
        limit=62,
    )(density, left_index, right_index, pair_count)

    def swap(value, axes, mask, size):
        return lax.ppermute(value, axes, [(i, i ^ mask) for i in range(size)])

    def row_swap(value, m):
        return swap(value, "row", m, 4)

    def col_swap(value):
        return swap(value, "col", 1, 2)

    def rep_swap(value):
        return swap(value, "rep", 1, 2)

    far, near, across = row_swap(payload, 2), row_swap(payload, 1), col_swap(payload)
    near_across, farthest = col_swap(near), row_swap(far, 1)
    far_across, farthest_across = col_swap(far), swap(far, ("row", "col"), 3, 8)
    own = [
        ((0, 0, 0), swap(payload, "rep", 0, 2)),
        ((1, 0, 0), near),
        ((1, 1, 0), near_across),
        ((0, 1, 0), across),
        ((2, 0, 0), far),
        ((3, 0, 0), farthest),
        ((2, 1, 0), far_across),
        ((3, 1, 0), farthest_across),
    ]
    pieces = [pair for (m, n, e), piece in own for pair in (((m, n, e), piece), ((m, n, 1), rep_swap(piece)))]
    offsets, pieces = zip(*pieces[::-1])
    current, codes = call(
        lambda *args: first_step_kernel(args[0], offsets, *args[1:]),
        sizes,
        [packed, jax.ShapeDtypeStruct(code_shape, jnp.int32)],
        [VMEM] * len(pieces),
        [VMEM] * 2,
        scratch(sizes.half),
    )(*pieces)
    return call(
        last_step_kernel,
        sizes,
        jax.ShapeDtypeStruct(density.shape, F32),
        [VMEM] * 2 + [ANY],
        VMEM,
        scratch(sizes.panel),
    )(current, rep_swap(current), codes)


def solution(mesh):
    def local(density, left_index, right_index, pair_count):
        sizes = Sizes(mesh.shape, density.shape[0], left_index.shape[3])
        fits = (
            (sizes.rows, sizes.cols, sizes.reps, sizes.slots, sizes.pairs) == (4, 2, 2, 8, 32)
            and density.shape[1:] == (64, 64)
        )
        if fits:
            return whole_form(sizes, density, left_index, right_index, pair_count)
        return panel_form(density, left_index, right_index, pair_count)

    in_specs = (
        P(("groups", "row", "col", "rep"), None, None),
        P(None, None, ("groups", "row", "col", "rep"), None),
        P(None, None, ("groups", "row", "col", "rep"), None),
        P(None, None, ("groups", "row", "col", "rep")),
    )
    out_specs = P(("groups", "row", "col", "rep"), None, None)
    return jax.shard_map(local, mesh=mesh, in_specs=in_specs, out_specs=out_specs, check_vma=False)
```
